512 devices in a mesh: grp: 8 (over x, y_hi), chan: 64 (over y_lo, z, core).
Axes of the slice: x: 4, y: 4 (y_hi: 2, y_lo: 2; y = y_hi * 2 + y_lo), z: 16, core: 2. Of those that a mesh axis runs over, the one named last changes fastest.
Arguments:
- voltages: bfloat16 [512, 1024, 1024], P('grp', 'chan'), may hold values from -6 to 6
- prototype: float32 [8, 1024], replicated, may hold values from -2 to 2
Outputs:
- visibilities: float32 [8, 5, 512, 2, 64, 64], P('grp', None, 'chan')
The draws below stay inside these ranges and needn't reach their ends.
All inputs are finite; a program needn't handle non-finite values.
Results may differ from the reference program's by a relative error of at most 0.0033.
Values may be sent and summed in bfloat16 or wider, within the bound.
A program may use at most 64 MiB of HBM per device.

```python
import math
import jax
import jax.numpy as jnp
from jax import lax

INPUTS = 512
CH = 512
TAPS = 8
FRAME = 1024
I_GRP = 64
SPECTRA = 1024
LAGS = 5
N_GRP = 8


def level_of(key, shape, split, low, high):
    def one(axis_at, parts):
        heights = jax.random.uniform(jax.random.fold_in(jax.random.fold_in(key, 6), axis_at), (parts,), jnp.float32, low / len(split), high / len(split))
        return jnp.repeat(jnp.exp(heights), shape[axis_at] // parts).reshape((-1,) + (1,) * (len(shape) - axis_at - 1))

    level = one(*split[0])
    for cut in split[1:]:
        level = level * one(*cut)
    return level


def scatter_about(rng, dims, width, bound, shards=(), kind=jnp.bfloat16):
    entries = width * jax.random.normal(rng, dims, jnp.float32)
    if shards:
        entries = entries * level_of(rng, dims, shards, -0.22, 0.18)
    return jnp.clip(entries, -bound, bound).astype(kind)


def setup_inputs(seed: int = 0) -> dict:
    streams_of = jax.random.split(jax.random.key(seed), 3)
    return {
        "voltages": scatter_about(streams_of[0], (INPUTS, SPECTRA, FRAME), 1.0, 6.0, ((0, 8), (1, 64))),
        "prototype": scatter_about(streams_of[1], (TAPS, FRAME), TAPS ** -0.5, 2.0, (), jnp.float32),
    }


def dft_table(frame_len, chan_count):
    sample = jnp.arange(frame_len, dtype=jnp.int32)[:, None]
    channel = jnp.arange(chan_count, dtype=jnp.int32)[None, :]
    phase = (sample * channel % frame_len).astype(jnp.float32) * (2.0 * math.pi / frame_len)
    scaling = 1.0 / math.sqrt(frame_len)
    table = jnp.stack([jnp.cos(phase) * scaling, -jnp.sin(phase) * scaling], axis=2)
    return table.reshape(frame_len, 2 * chan_count).astype(jnp.bfloat16)

def channelize(samples, prototype, table):
    tap_count = prototype.shape[0]
    spec_count = samples.shape[1]
    padding = jnp.zeros((samples.shape[0], tap_count - 1, samples.shape[2]), jnp.bfloat16)
    padded = jnp.concatenate([padding, samples], axis=1)
    filtered = jnp.zeros(samples.shape, jnp.float32)
    for offset in range(tap_count):
        filtered = filtered + prototype[offset][None, None, :] * padded[:, offset:offset + spec_count, :].astype(jnp.float32)
    filtered = filtered.astype(jnp.bfloat16)
    spectra = jnp.einsum('isn,nq->qsi', filtered.astype(jnp.float32), table.astype(jnp.float32), precision=lax.Precision.HIGHEST).astype(jnp.bfloat16)
    return spectra.reshape(spectra.shape[0] // 2, 2, spec_count, samples.shape[0])

def reference(voltages, prototype):
    table = dft_table(FRAME, CH)
    grouped = voltages.reshape(N_GRP, I_GRP, SPECTRA, FRAME)
    spectra = lax.map(lambda block: channelize(block, prototype, table), grouped)
    scaling = 1.0 / math.sqrt(SPECTRA)

    def per_group(group):
        own = spectra[group].astype(jnp.float32)
        flipped = jnp.stack([own[:, 1], -own[:, 0]], axis=1)
        results = []
        for lag in range(LAGS):
            partner = spectra[(group - lag) % N_GRP].astype(jnp.float32)
            real_part = jnp.einsum('cpsi,cpsj->cij', own, partner, precision=lax.Precision.HIGHEST)
            imag_part = jnp.einsum('cpsi,cpsj->cij', flipped, partner, precision=lax.Precision.HIGHEST)
            results.append(jnp.stack([real_part, imag_part], axis=1) * scaling)
        return jnp.stack(results, axis=0)
    return lax.map(per_group, jnp.arange(N_GRP, dtype=jnp.int32))
```

```python
import math

import jax
import jax.numpy as jnp
import numpy as np
from jax import lax
from jax.experimental import pallas as pl
from jax.experimental.pallas import tpu as pltpu
from jax.sharding import PartitionSpec as P

MESH = pl.DeviceIdType.MESH
BF16, F32 = jnp.bfloat16, jnp.float32

TAPS, FRAME, INP, SPEC = 8, 1024, 64, 16
NZ, NM, NG, NL = 16, 32, 8, 5
BACK, AHEAD = 4, 3
ROLES = [8] + [s * r for r in range(7, 0, -1) for s in (1, -1)] + [0]
HUB = 3


def hub_of(role):
    return 0 if abs(role) < 2 else (HUB if role > 0 else -HUB)


SIDE_A = [r for r in ROLES if hub_of(r) == HUB and r != HUB]
SIDE_B = [r for r in ROLES if hub_of(r) == -HUB and r != -HUB]
SIDE_C = [r for r in ROLES if hub_of(r) == 0 and r != 0]


def dft_table():
    m = np.arange(NM)
    plane = np.arange(NZ)[:, None]
    chan = (((m // 2) % 2) * NZ + plane) * 2 + m % 2
    k = 8 * chan + m // 4
    phase = (k[:, :, None] * np.arange(FRAME)) % FRAME * (2.0 * np.pi / FRAME)
    table = np.stack([np.cos(phase), -np.sin(phase)], axis=1) / math.sqrt(FRAME)
    table = table.reshape(NZ, 2, NM // 2, 2, FRAME).transpose(0, 3, 1, 2, 4)
    return table.reshape(NZ, 2, NM, FRAME).astype(jnp.bfloat16)


def kernel(volt, proto, table, out, vt, hs, hr, filt, stage, sendp, recvp, za, zb, zc, pa, pb, qa, qb, fin, rr,
           hsem, hrsem, psem, prsem, zsem, zrsem, qsem, qrsem, rsem, rrsem):
    grp = lax.axis_index("grp")
    chan = lax.axis_index("chan")
    core = lax.rem(chan, 2)
    z = lax.rem(chan // 2, NZ)
    ylo = chan // (2 * NZ)
    mine = grp * 4 + ylo * 2 + core
    sgn = 1 - 2 * core

    def in_plane(m):
        return (m // 4, (lax.rem(m // 2, 2) * NZ + z) * 2 + lax.rem(m, 2))

    def in_column(offset):
        return (grp, (ylo * NZ + lax.rem(z + offset + 2 * NZ, NZ)) * 2 + core)

    after = (grp, lax.rem(chan + 1, 64))
    before = (grp, lax.rem(chan + 63, 64))
    beyond = (grp, lax.rem(chan + 63 + 2 * core, 64))

    barrier = pltpu.get_barrier_semaphore()

    @pl.loop(1, NM)
    def _(k):
        pl.semaphore_signal(barrier, inc=1, device_id=in_plane(lax.rem(mine + k, NM)), device_id_type=MESH)

    for d in (1, 2, 3, 4, 5):
        for s in (1, -1):
            pl.semaphore_signal(barrier, inc=1, device_id=in_column(s * d), device_id_type=MESH)
    pl.semaphore_signal(barrier, inc=1, device_id=beyond, device_id_type=MESH)

    @pl.loop(0, INP)
    def _(i):
        for nt in range(8):
            tile = volt[i, :, nt * 128:(nt + 1) * 128].astype(F32)
            vt[nt, pl.ds(BACK * INP + i, SPEC, stride=INP), :] = tile

    @pl.loop(0, 8)
    def _(nt):
        for n, f in enumerate([16, 17, 18, 19, 4, 5, 6]):
            hs[n, nt] = vt[nt, f * INP:(f + 1) * INP, :].astype(BF16)

    pl.semaphore_wait(barrier, NM - 1 + 11)
    forward = pltpu.make_async_remote_copy(
        src_ref=hs.at[0:BACK], dst_ref=hr.at[0:BACK], send_sem=hsem.at[0], recv_sem=hrsem.at[0],
        device_id=after, device_id_type=MESH)
    backward = pltpu.make_async_remote_copy(
        src_ref=hs.at[BACK:7], dst_ref=hr.at[BACK:7], send_sem=hsem.at[1], recv_sem=hrsem.at[1],
        device_id=before, device_id_type=MESH)
    forward.start()
    backward.start()

    last = jnp.where(chan == 63, 0.0, 1.0).astype(F32)
    first = jnp.where(chan == 0, 0.0, 1.0).astype(F32)

    def fir(lo, hi, masked):
        @pl.loop(0, 32)
        def _(idx):
            nt = idx // 4
            row = lax.rem(idx, 4) * 16
            lanes = pl.ds(pl.multiple_of(nt * 128, 128), 128)
            taps = [proto[t:t + 1, lanes] for t in range(TAPS)]
            frames = {}
            for f in range(lo, hi + TAPS - 1):
                value = vt[nt, pl.ds(pl.multiple_of(f * INP + row, 16), 16), :]
                frames[f] = value * last if masked and f < BACK + SPEC else value
            for j in range(lo, hi):
                total = taps[0] * frames[j]
                for t in range(1, TAPS):
                    total = total + taps[t] * frames[j + t]
                filt[pl.ds(pl.multiple_of(j * INP + row, 16), 16), lanes] = total.astype(BF16)

    fir(BACK, SPEC - AHEAD, False)

    low = lax.broadcasted_iota(jnp.int32, (NM // 2, 128), 1) < 64

    def dft(ch, groups):
        lhs = jnp.concatenate(
            [table[lax.rem(z + s * ROLES[u] + NZ, NZ), (s + 1) // 2] for u in range(4 * ch, 4 * ch + 4) for s in (-1, 1)],
            axis=0)
        for sg in groups:
            full = lax.dot_general(lhs, filt[sg * 256:(sg + 1) * 256, :], (((1,), (1,)), ((), ())),
                                   preferred_element_type=F32)
            for uc in range(8):
                for s2 in range(2):
                    re = full[uc * 32:uc * 32 + 16, s2 * 128:(s2 + 1) * 128]
                    im = full[uc * 32 + 16:uc * 32 + 32, s2 * 128:(s2 + 1) * 128]
                    even = jnp.where(low, re, pltpu.roll(im, 64, 1))
                    odd = jnp.where(low, pltpu.roll(re, 64, 1), im)
                    row = ((uc // 2) * NM + uc % 2) * SPEC + sg * 4 + s2 * 2
                    stage[pl.ds(row, NM // 2, stride=2 * SPEC), :] = even
                    stage[pl.ds(row + 1, NM // 2, stride=2 * SPEC), :] = odd

    def send_plane(ch):
        @pl.loop(0, NM)
        def _(m):
            for u in range(4):
                start = pl.multiple_of((u * NM + m) * SPEC, SPEC)
                sendp[4 * ch + u, m] = stage[pl.ds(start, SPEC), :].astype(BF16)

        own = pltpu.make_async_copy(sendp.at[4 * ch:4 * ch + 4, mine], recvp.at[4 * ch:4 * ch + 4, mine], prsem.at[ch])
        own.start()

        @pl.loop(1, NM)
        def _(k):
            m = lax.rem(mine + k, NM)
            pltpu.make_async_remote_copy(
                src_ref=sendp.at[4 * ch:4 * ch + 4, m], dst_ref=recvp.at[4 * ch:4 * ch + 4, mine],
                send_sem=psem, recv_sem=prsem.at[ch], device_id=in_plane(m), device_id_type=MESH).start()

    def send_column(ch):
        block = recvp.at[4 * ch:4 * ch + 4]
        pltpu.make_async_copy(block, block, prsem.at[ch]).wait()
        for u in range(4 * ch, 4 * ch + 4):
            role = ROLES[u]
            hub = hub_of(role)
            if role == hub:
                continue
            side = 0 if hub > 0 else (1 if hub < 0 else 2)
            slot = (SIDE_A, SIDE_B, SIDE_C)[side].index(role)
            pltpu.make_async_remote_copy(
                src_ref=recvp.at[u], dst_ref=(za, zb, zc)[side].at[slot], send_sem=zsem, recv_sem=zrsem.at[side],
                device_id=in_column(sgn * (hub - role)), device_id_type=MESH).start()

    dft(0, (1, 2))
    forward.wait_recv()
    backward.wait_recv()

    @pl.loop(0, 8)
    def _(nt):
        for n, f in enumerate([0, 1, 2, 3, 20, 21, 22]):
            value = hr[n, nt].astype(F32)
            vt[nt, f * INP:(f + 1) * INP, :] = value * first if f < BACK else value

    fir(0, BACK, False)
    fir(SPEC - AHEAD, SPEC, True)
    dft(0, (0, 3))
    send_plane(0)
    dft(1, range(4))
    send_plane(1)
    send_column(0)
    dft(2, range(4))
    send_plane(2)
    send_column(1)
    dft(3, range(4))
    send_plane(3)
    send_column(2)
    send_column(3)

    flip = jnp.where(lax.broadcasted_iota(jnp.int32, (64, 128), 1) < 64, 1.0, -1.0).astype(F32)

    def group_rows(g, held, own):
        planes = held.shape[0]
        part = pl.ds(g * 4, 4)
        return jnp.concatenate(
            [held[:, part].reshape(planes * 64, 128), recvp[own, part].reshape(64, 128)], axis=0)

    def products(w, held, role, lags):
        own = ROLES.index(role)
        left = group_rows(lax.rem(grp + 1 + w, NG), held, own)
        right = [left] + [group_rows(lax.rem(grp + 1 + w - lag + NG, NG), held, own) for lag in range(1, lags)]
        full = lax.dot_general(left, jnp.concatenate(right, axis=1), (((0,), (0,)), ((), ())),
                               preferred_element_type=F32)
        blocks = []
        for lag in range(lags):
            part = full[:, lag * 128:(lag + 1) * 128]
            blocks.append(part[0:64] * flip + pltpu.roll(part[64:128], 64, 1))
        return blocks

    def partial(w, lags, held, role, sums, landing, side, offset):
        for lag, block in enumerate(products(w, held, role, lags)):
            sums[w, lag] = block.astype(BF16)
        pltpu.make_async_remote_copy(
            src_ref=sums.at[w, 0:lags], dst_ref=landing.at[w, 0:lags], send_sem=qsem, recv_sem=qrsem.at[side, w],
            device_id=in_column(offset), device_id_type=MESH).start()

    pltpu.make_async_copy(za, za, zrsem.at[0]).wait()
    pltpu.make_async_copy(zb, zb, zrsem.at[1]).wait()
    for base, lags in ((0, 5), (4, 4)):
        @pl.loop(base, base + 4)
        def _(w):
            partial(w, lags, za, HUB, pa, qa, 0, -sgn * HUB)
            partial(w, lags, zb, -HUB, pb, qb, 1, sgn * HUB)

    pltpu.make_async_copy(zc, zc, zrsem.at[2]).wait()
    scale = 1.0 / 32.0

    def reply(w):
        return pltpu.make_async_remote_copy(
            src_ref=fin.at[w], dst_ref=rr.at[w], send_sem=rsem, recv_sem=rrsem.at[w],
            device_id=(lax.rem(grp + 1 + w, NG), chan), device_id_type=MESH)

    def finish(w, lags):
        for side, landing in ((0, qa), (1, qb)):
            here = landing.at[w, 0:lags]
            pltpu.make_async_copy(here, here, qrsem.at[side, w]).wait()
        for lag, block in enumerate(products(w, zc, 0, lags)):
            fin[w, lag] = (block + qa[w, lag].astype(F32) + qb[w, lag].astype(F32)) * scale
        if lags < NL:
            other = fin[w - 4, 4]
            square = jnp.concatenate([other, pltpu.roll(other, 64, 1)], axis=0)
            fin[w, 4] = square.T[0:64] * flip

    @pl.loop(0, 4)
    def _(w):
        finish(w, 5)
        reply(w).start()

    @pl.loop(4, 7)
    def _(w):
        finish(w, 4)
        reply(w).start()

    finish(7, 4)

    def deliver(w, source):
        c8 = lax.rem(grp - 1 - w + 2 * NG, NG)
        for lag in range(NL):
            block = source[w, lag]
            out[0, lag, c8, 0] = block[:, 0:64]
            out[0, lag, c8, 1] = pltpu.roll(block, 64, 1)[:, 0:64]

    deliver(7, fin)

    @pl.loop(0, 7)
    def _(w):
        pltpu.make_async_copy(rr.at[w], rr.at[w], rrsem.at[w]).wait()
        deliver(w, rr)

    forward.wait_send()
    backward.wait_send()

    def drain(ref, sem):
        pltpu.make_async_copy(ref, ref, sem).wait()

    drain(sendp.at[:, 0:NM - 1], psem)
    drain(recvp.at[0:len(SIDE_A) + len(SIDE_B) + len(SIDE_C)], zsem)
    for sums in (pa, pb):
        drain(sums.at[0:4], qsem)
        drain(sums.at[4:8, 0:4], qsem)
    drain(fin.at[0:7], rsem)


def shards(voltages, prototype):
    call = pl.pallas_call(
        kernel,
        out_shape=jax.ShapeDtypeStruct((1, NL, NG, 2, 64, 64), F32),
        in_specs=[pl.BlockSpec(memory_space=pltpu.VMEM)] * 3,
        out_specs=pl.BlockSpec(memory_space=pltpu.VMEM),
        scratch_shapes=[
            pltpu.VMEM((8, 24 * INP, 128), F32),
            pltpu.VMEM((7, 8, INP, 128), BF16),
            pltpu.VMEM((7, 8, INP, 128), BF16),
            pltpu.VMEM((SPEC * INP, FRAME), BF16),
            pltpu.VMEM((4 * NM * SPEC, 128), F32),
            pltpu.VMEM((NZ, NM, SPEC, 128), BF16),
            pltpu.VMEM((NZ, NM, SPEC, 128), BF16),
            pltpu.VMEM((len(SIDE_A), NM, SPEC, 128), BF16),
            pltpu.VMEM((len(SIDE_B), NM, SPEC, 128), BF16),
            pltpu.VMEM((len(SIDE_C), NM, SPEC, 128), BF16),
            pltpu.VMEM((8, NL, 64, 128), BF16),
            pltpu.VMEM((8, NL, 64, 128), BF16),
            pltpu.VMEM((8, NL, 64, 128), BF16),
            pltpu.VMEM((8, NL, 64, 128), BF16),
            pltpu.VMEM((8, NL, 64, 128), F32),
            pltpu.VMEM((8, NL, 64, 128), F32),
            pltpu.SemaphoreType.DMA((2,)),
            pltpu.SemaphoreType.DMA((2,)),
            pltpu.SemaphoreType.DMA,
            pltpu.SemaphoreType.DMA((4,)),
            pltpu.SemaphoreType.DMA,
            pltpu.SemaphoreType.DMA((3,)),
            pltpu.SemaphoreType.DMA,
            pltpu.SemaphoreType.DMA((2, 8)),
            pltpu.SemaphoreType.DMA,
            pltpu.SemaphoreType.DMA((8,)),
        ],
        compiler_params=pltpu.CompilerParams(
            collective_id=0, has_side_effects=True, vmem_limit_bytes=56 << 20),
        cost_estimate=pl.CostEstimate(flops=4_000_000_000, bytes_accessed=8_000_000, transcendentals=0),
        name="fx",
    )
    return call(voltages, prototype, jnp.asarray(dft_table()))


def solution(mesh):
    in_specs = (P("grp", "chan", None), P())
    out_specs = P("grp", None, "chan", None, None, None)
    return jax.shard_map(shards, mesh=mesh, in_specs=in_specs, out_specs=out_specs, check_vma=False)
```

```python
import math

import jax
import jax.numpy as jnp
import numpy as np
from jax import lax
from jax.experimental import pallas as pl
from jax.experimental.pallas import tpu as pltpu
from jax.sharding import PartitionSpec as P

MESH = pl.DeviceIdType.MESH
BF16, F32 = jnp.bfloat16, jnp.float32

TAPS, FRAME, INP, SPEC = 8, 1024, 64, 16
NZ, NM, NG, NL = 16, 32, 8, 5
BACK, AHEAD = 4, 3
ROLES = [7, -7, 8] + [s * r for r in range(6, 0, -1) for s in (1, -1)] + [0]
HUB = 3
DIRECT = 2
CHUNKS = ((2, 4), (4, 8), (8, 12), (12, 16))


def hub_of(role):
    return 0 if abs(role) < 2 else (HUB if role > 0 else -HUB)


SIDE_A = [r for r in ROLES if hub_of(r) == HUB and r != HUB]
SIDE_B = [r for r in ROLES if hub_of(r) == -HUB and r != -HUB]
SIDE_C = [r for r in ROLES if hub_of(r) == 0 and r != 0]


def dft_table():
    m = np.arange(NM)
    plane = np.arange(NZ)[:, None]
    chan = (((m // 2) % 2) * NZ + plane) * 2 + m % 2
    k = 8 * chan + m // 4
    phase = (k[:, :, None] * np.arange(FRAME)) % FRAME * (2.0 * np.pi / FRAME)
    table = np.stack([np.cos(phase), -np.sin(phase)], axis=1) / math.sqrt(FRAME)
    table = table.reshape(NZ, 2, NM // 2, 2, FRAME).transpose(0, 3, 1, 2, 4)
    return table.reshape(NZ, 2, NM, FRAME).astype(jnp.bfloat16)


def kernel(volt_hbm, proto, table_hbm, out, volt, table, vt, hs, hr, filt, stage, sendp, recvp, za, zb, zc,
           pa, pb, qa, qb, fin, plane_in, insem, hsem, hrsem, psem, prsem, zsem, zrsem, qsem, qrsem, rsem, rrsem):
    grp = lax.axis_index("grp")
    chan = lax.axis_index("chan")
    core = lax.rem(chan, 2)
    z = lax.rem(chan // 2, NZ)
    ylo = chan // (2 * NZ)
    mine = grp * 4 + ylo * 2 + core
    sgn = 1 - 2 * core

    def in_plane(m, offset=0):
        return (m // 4, (lax.rem(m // 2, 2) * NZ + lax.rem(z + offset + NZ, NZ)) * 2 + lax.rem(m, 2))

    def in_column(offset):
        return (grp, (ylo * NZ + lax.rem(z + offset + 2 * NZ, NZ)) * 2 + core)

    after = (grp, lax.rem(chan + 1, 64))
    before = (grp, lax.rem(chan + 63, 64))
    beyond = (grp, lax.rem(chan + 63 + 2 * core, 64))

    fetches = [
        pltpu.make_async_copy(volt_hbm.at[n * 16:(n + 1) * 16], volt.at[n * 16:(n + 1) * 16], insem.at[n])
        for n in range(4)
    ]
    fetch_table = pltpu.make_async_copy(table_hbm, table, insem.at[4])
    for fetch in fetches:
        fetch.start()
    barrier = pltpu.get_barrier_semaphore()

    @pl.loop(1, NM)
    def _(k):
        pl.semaphore_signal(barrier, inc=1, device_id=in_plane(lax.rem(mine + k, NM)), device_id_type=MESH)

    for d in (1, 2, 3, 4, 5):
        for s in (1, -1):
            pl.semaphore_signal(barrier, inc=1, device_id=in_column(s * d), device_id_type=MESH)
    pl.semaphore_signal(barrier, inc=1, device_id=beyond, device_id_type=MESH)

    for n in range(4):
        fetches[n].wait()
        if n == 3:
            fetch_table.start()

        @pl.loop(n * 16, (n + 1) * 16)
        def _(i):
            for nt in range(8):
                tile = volt[i, :, nt * 128:(nt + 1) * 128].astype(F32)
                vt[nt, pl.ds(BACK * INP + i, SPEC, stride=INP), :] = tile

    @pl.loop(0, 8)
    def _(nt):
        for n, f in enumerate([16, 17, 18, 19, 4, 5, 6]):
            hs[n, nt] = vt[nt, f * INP:(f + 1) * INP, :].astype(BF16)

    pl.semaphore_wait(barrier, NM - 1 + 11)
    for offset in (HUB - 7, 7 - HUB):
        pl.semaphore_signal(plane_in, inc=1, device_id=in_column(offset), device_id_type=MESH)
    forward = pltpu.make_async_remote_copy(
        src_ref=hs.at[0:BACK], dst_ref=hr.at[0:BACK], send_sem=hsem.at[0], recv_sem=hrsem.at[0],
        device_id=after, device_id_type=MESH)
    backward = pltpu.make_async_remote_copy(
        src_ref=hs.at[BACK:7], dst_ref=hr.at[BACK:7], send_sem=hsem.at[1], recv_sem=hrsem.at[1],
        device_id=before, device_id_type=MESH)
    forward.start()
    backward.start()

    last = jnp.where(chan == 63, 0.0, 1.0).astype(F32)
    first = jnp.where(chan == 0, 0.0, 1.0).astype(F32)

    def fir(lo, hi, masked):
        @pl.loop(0, 32)
        def _(idx):
            nt = idx // 4
            row = lax.rem(idx, 4) * 16
            lanes = pl.ds(pl.multiple_of(nt * 128, 128), 128)
            taps = [proto[t:t + 1, lanes] for t in range(TAPS)]
            frames = {}
            for f in range(lo, hi + TAPS - 1):
                value = vt[nt, pl.ds(pl.multiple_of(f * INP + row, 16), 16), :]
                frames[f] = value * last if masked and f < BACK + SPEC else value
            for j in range(lo, hi):
                total = taps[0] * frames[j]
                for t in range(1, TAPS):
                    total = total + taps[t] * frames[j + t]
                filt[pl.ds(pl.multiple_of(j * INP + row, 16), 16), lanes] = total.astype(BF16)

    fir(BACK, SPEC - AHEAD, False)

    low = lax.broadcasted_iota(jnp.int32, (NM // 2, 128), 1) < 64

    def dft(first_u, last_u, groups):
        lhs = jnp.concatenate(
            [table[lax.rem(z + s * ROLES[u] + NZ, NZ), (s + 1) // 2] for u in range(first_u, last_u) for s in (-1, 1)],
            axis=0)
        for sg in groups:
            full = lax.dot_general(lhs, filt[sg * 256:(sg + 1) * 256, :], (((1,), (1,)), ((), ())),
                                   preferred_element_type=F32)
            for uc in range(2 * (last_u - first_u)):
                for s2 in range(2):
                    re = full[uc * 32:uc * 32 + 16, s2 * 128:(s2 + 1) * 128]
                    im = full[uc * 32 + 16:uc * 32 + 32, s2 * 128:(s2 + 1) * 128]
                    even = jnp.where(low, re, pltpu.roll(im, 64, 1))
                    odd = jnp.where(low, pltpu.roll(re, 64, 1), im)
                    row = ((first_u + uc // 2) * NM + uc % 2) * SPEC + sg * 4 + s2 * 2
                    stage[pl.ds(row, NM // 2, stride=2 * SPEC), :] = even
                    stage[pl.ds(row + 1, NM // 2, stride=2 * SPEC), :] = odd

    def pack(lo, hi):
        @pl.loop(0, NM)
        def _(m):
            for u in range(lo, hi):
                start = pl.multiple_of((u * NM + m) * SPEC, SPEC)
                sendp[u, m] = stage[pl.ds(start, SPEC), :].astype(BF16)

    def send_direct():
        pack(0, DIRECT)
        pl.semaphore_wait(plane_in, 2)

        @pl.loop(0, NM)
        def _(k):
            m = lax.rem(mine + k, NM)
            for u in range(DIRECT):
                side = 0 if ROLES[u] > 0 else 1
                slot = (SIDE_A, SIDE_B)[side].index(ROLES[u])
                offset = (1 - 2 * lax.rem(m, 2)) * (hub_of(ROLES[u]) - ROLES[u])
                pltpu.make_async_remote_copy(
                    src_ref=sendp.at[u, m], dst_ref=(za, zb)[side].at[slot, mine], send_sem=zsem,
                    recv_sem=zrsem.at[side], device_id=in_plane(m, offset), device_id_type=MESH).start()

    def send_plane(ch):
        lo, hi = CHUNKS[ch]
        pack(lo, hi)
        pltpu.make_async_copy(sendp.at[lo:hi, mine], recvp.at[lo:hi, mine], prsem.at[ch]).start()

        @pl.loop(1, NM)
        def _(k):
            m = lax.rem(mine + k, NM)
            pltpu.make_async_remote_copy(
                src_ref=sendp.at[lo:hi, m], dst_ref=recvp.at[lo:hi, mine],
                send_sem=psem, recv_sem=prsem.at[ch], device_id=in_plane(m), device_id_type=MESH).start()

    def send_column(ch):
        lo, hi = CHUNKS[ch]
        block = recvp.at[lo:hi]
        pltpu.make_async_copy(block, block, prsem.at[ch]).wait()
        for u in range(lo, hi):
            role = ROLES[u]
            hub = hub_of(role)
            if role == hub:
                continue
            side = 0 if hub > 0 else (1 if hub < 0 else 2)
            slot = (SIDE_A, SIDE_B, SIDE_C)[side].index(role)
            pltpu.make_async_remote_copy(
                src_ref=recvp.at[u], dst_ref=(za, zb, zc)[side].at[slot], send_sem=zsem, recv_sem=zrsem.at[side],
                device_id=in_column(sgn * (hub - role)), device_id_type=MESH).start()

    fetch_table.wait()
    for u in range(0, NZ, 4):
        dft(u, u + 4, (1, 2))
    forward.wait_recv()
    backward.wait_recv()

    @pl.loop(0, 8)
    def _(nt):
        for n, f in enumerate([0, 1, 2, 3, 20, 21, 22]):
            value = hr[n, nt].astype(F32)
            vt[nt, f * INP:(f + 1) * INP, :] = value * first if f < BACK else value

    fir(0, BACK, False)
    fir(SPEC - AHEAD, SPEC, True)
    dft(0, DIRECT, (0, 3))
    send_direct()
    for ch, (lo, hi) in enumerate(CHUNKS):
        dft(lo, hi, (0, 3))
        send_plane(ch)
        if ch:
            send_column(ch - 1)
    send_column(len(CHUNKS) - 1)

    flip = jnp.where(lax.broadcasted_iota(jnp.int32, (64, 128), 1) < 64, 1.0, -1.0).astype(F32)

    def group_rows(g, held, own):
        planes = held.shape[0]
        part = pl.ds(g * 4, 4)
        return jnp.concatenate(
            [held[:, part].reshape(planes * 64, 128), recvp[own, part].reshape(64, 128)], axis=0)

    def products(w, held, role, lags):
        own = ROLES.index(role)
        left = group_rows(lax.rem(grp + 1 + w, NG), held, own)
        right = [left] + [group_rows(lax.rem(grp + 1 + w - lag + NG, NG), held, own) for lag in range(1, lags)]
        full = lax.dot_general(left, jnp.concatenate(right, axis=1), (((0,), (0,)), ((), ())),
                               preferred_element_type=F32)
        blocks = []
        for lag in range(lags):
            part = full[:, lag * 128:(lag + 1) * 128]
            blocks.append(part[0:64] * flip + pltpu.roll(part[64:128], 64, 1))
        return blocks

    row = lax.broadcasted_iota(jnp.int32, (64, 128), 0)
    lane = lax.broadcasted_iota(jnp.int32, (64, 128), 1)
    left_half = lane < 64
    column = jnp.where(left_half, lane, lane - 64)

    def folded(one, two):
        lower = row >= column
        return jnp.where(left_half, jnp.where(lower, one, pltpu.roll(one, 64, 1)),
                         jnp.where(lower, pltpu.roll(two, 64, 1), two))

    def unfolded(value):
        both = jnp.where(left_half, value, pltpu.roll(value, 64, 1))
        turned = jnp.concatenate([value, value], axis=0).T[0:64]
        real = jnp.where(row >= column, both, turned)
        imag = jnp.where(row < column, both, jnp.where(row > column, -turned, 0.0))
        return jnp.where(left_half, real, imag)

    def partial(pair, lags, held, role, sums, landing, side, offset):
        diagonal = []
        for half in range(2):
            blocks = products(pair + half, held, role, lags)
            diagonal.append(blocks[0])
            for lag in range(1, lags):
                sums[pair + half, lag - 1] = blocks[lag].astype(BF16)
        sums[pair, lags - 1] = folded(*diagonal).astype(BF16)
        for half in range(2):
            w = pair + half
            pltpu.make_async_remote_copy(
                src_ref=sums.at[w, 0:lags - half], dst_ref=landing.at[w, 0:lags - half], send_sem=qsem,
                recv_sem=qrsem.at[side, w], device_id=in_column(offset), device_id_type=MESH).start()

    pltpu.make_async_copy(za, za, zrsem.at[0]).wait()
    pltpu.make_async_copy(zb, zb, zrsem.at[1]).wait()
    for base, lags in ((0, 5), (4, 4)):
        @pl.loop(0, 2)
        def _(p):
            partial(base + 2 * p, lags, za, HUB, pa, qa, 0, -sgn * HUB)
            partial(base + 2 * p, lags, zb, -HUB, pb, qb, 1, sgn * HUB)

    pltpu.make_async_copy(zc, zc, zrsem.at[2]).wait()
    for base, lags in ((0, 5), (4, 4)):
        @pl.loop(base, base + 4)
        def _(w):
            for lag, block in enumerate(products(w, zc, 0, lags)):
                fin[w, lag] = block

    scale = 1.0 / 32.0

    def reply(w):
        pltpu.make_async_remote_copy(
            src_ref=fin.at[w], dst_ref=out.at[grp], send_sem=rsem, recv_sem=rrsem.at[w],
            device_id=(lax.rem(grp + 1 + w, NG), chan), device_id_type=MESH).start()

    def finish(pair, lags):
        for half in range(2):
            w = pair + half
            for side, landing in ((0, qa), (1, qb)):
                here = landing.at[w, 0:lags - half]
                pltpu.make_async_copy(here, here, qrsem.at[side, w]).wait()
            for lag in range(1, lags):
                fin[w, lag] = (fin[w, lag] + qa[w, lag - 1].astype(F32) + qb[w, lag - 1].astype(F32)) * scale
            if lags == NL:
                other = fin[w, 4]
                square = jnp.concatenate([other, pltpu.roll(other, 64, 1)], axis=0)
                fin[w + 4, 4] = square.T[0:64] * flip
            if not half:
                packed = qa[w, lags - 1].astype(F32) + qb[w, lags - 1].astype(F32)
                fin[w, 0] = (fin[w, 0] + unfolded(packed)) * scale
                fin[w + 1, 0] = (fin[w + 1, 0] + unfolded(pltpu.roll(packed, 64, 1))) * scale
            if not (isinstance(w, int) and w == 7):
                reply(w)

    @pl.loop(0, 2)
    def _(p):
        finish(2 * p, 5)

    finish(4, 4)
    finish(6, 4)
    keep = pltpu.make_async_copy(fin.at[7], out.at[grp], insem.at[0])
    keep.start()
    for w in range(7):
        here = out.at[lax.rem(grp - 1 - w + 2 * NG, NG)]
        pltpu.make_async_copy(here, here, rrsem.at[w]).wait()
    keep.wait()

    forward.wait_send()
    backward.wait_send()

    def drain(ref, sem):
        pltpu.make_async_copy(ref, ref, sem).wait()

    drain(sendp.at[DIRECT:, 0:NM - 1], psem)
    drain(recvp.at[0:len(SIDE_A) + len(SIDE_B) + len(SIDE_C)], zsem)
    for sums in (pa, pb):
        drain(sums.at[0:8, 0:4], qsem)
    drain(fin.at[0:7], rsem)


def split(packed, out, held, parts, insem, outsem):
    def fetch(n):
        return pltpu.make_async_copy(packed.at[n], held.at[n], insem.at[n])

    for n in range(NG):
        fetch(n).start()
    for n in range(NG):
        fetch(n).wait()
        value = held[n]
        parts[:, n, 0] = value[:, :, 0:64]
        parts[:, n, 1] = pltpu.roll(value, 64, 2)[:, :, 0:64]
        pltpu.make_async_copy(parts.at[:, n], out.at[0, :, n], outsem).start()
    pltpu.make_async_copy(parts, out.at[0], outsem).wait()


def shards(voltages, prototype):
    anywhere = pl.BlockSpec(memory_space=pl.ANY)
    call = pl.pallas_call(
        kernel,
        out_shape=jax.ShapeDtypeStruct((NG, NL, 64, 128), F32),
        in_specs=[anywhere, pl.BlockSpec(memory_space=pltpu.VMEM), anywhere],
        out_specs=anywhere,
        scratch_shapes=[
            pltpu.VMEM((INP, SPEC, FRAME), BF16),
            pltpu.VMEM((NZ, 2, NM, FRAME), BF16),
            pltpu.VMEM((8, 24 * INP, 128), F32),
            pltpu.VMEM((7, 8, INP, 128), BF16),
            pltpu.VMEM((7, 8, INP, 128), BF16),
            pltpu.VMEM((SPEC * INP, FRAME), BF16),
            pltpu.VMEM((NZ * NM * SPEC, 128), F32),
            pltpu.VMEM((NZ, NM, SPEC, 128), BF16),
            pltpu.VMEM((NZ, NM, SPEC, 128), BF16),
            pltpu.VMEM((len(SIDE_A), NM, SPEC, 128), BF16),
            pltpu.VMEM((len(SIDE_B), NM, SPEC, 128), BF16),
            pltpu.VMEM((len(SIDE_C), NM, SPEC, 128), BF16),
            pltpu.VMEM((8, NL, 64, 128), BF16),
            pltpu.VMEM((8, NL, 64, 128), BF16),
            pltpu.VMEM((8, NL, 64, 128), BF16),
            pltpu.VMEM((8, NL, 64, 128), BF16),
            pltpu.VMEM((8, NL, 64, 128), F32),
            pltpu.SemaphoreType.REGULAR,
            pltpu.SemaphoreType.DMA((5,)),
            pltpu.SemaphoreType.DMA((2,)),
            pltpu.SemaphoreType.DMA((2,)),
            pltpu.SemaphoreType.DMA,
            pltpu.SemaphoreType.DMA((len(CHUNKS),)),
            pltpu.SemaphoreType.DMA,
            pltpu.SemaphoreType.DMA((3,)),
            pltpu.SemaphoreType.DMA,
            pltpu.SemaphoreType.DMA((2, 8)),
            pltpu.SemaphoreType.DMA,
            pltpu.SemaphoreType.DMA((7,)),
        ],
        compiler_params=pltpu.CompilerParams(
            collective_id=0, has_side_effects=True, vmem_limit_bytes=56 << 20),
        cost_estimate=pl.CostEstimate(flops=4_000_000_000, bytes_accessed=8_000_000, transcendentals=0),
        name="fx",
    )
    packed = call(voltages, prototype, jnp.asarray(dft_table()))
    return pl.pallas_call(
        split,
        out_shape=jax.ShapeDtypeStruct((1, NL, NG, 2, 64, 64), F32),
        in_specs=[anywhere],
        out_specs=anywhere,
        scratch_shapes=[
            pltpu.VMEM((NG, NL, 64, 128), F32),
            pltpu.VMEM((NL, NG, 2, 64, 64), F32),
            pltpu.SemaphoreType.DMA((NG,)),
            pltpu.SemaphoreType.DMA,
        ],
        cost_estimate=pl.CostEstimate(flops=0, bytes_accessed=4_000_000, transcendentals=0),
        name="split",
    )(packed)


def solution(mesh):
    in_specs = (P("grp", "chan", None), P())
    out_specs = P("grp", None, "chan", None, None, None)
    return jax.shard_map(shards, mesh=mesh, in_specs=in_specs, out_specs=out_specs, check_vma=False)
```

```python
import math

import jax
import jax.numpy as jnp
import numpy as np
from jax import lax
from jax.experimental import pallas as pl
from jax.experimental.pallas import tpu as pltpu
from jax.sharding import PartitionSpec as P

MESH = pl.DeviceIdType.MESH
BF16, F32 = jnp.bfloat16, jnp.float32

TAPS, FRAME, INP, SPEC = 8, 1024, 64, 16
NZ, NM, NG, NL = 16, 32, 8, 5
BACK, AHEAD = 4, 3
ROLES = [7, -7, 8] + [s * r for r in range(6, 0, -1) for s in (1, -1)] + [0]
HUB = 3
DIRECT = 2
CHUNKS = ((2, 4), (4, 8), (8, 12), (12, 16))


def hub_of(role):
    return 0 if abs(role) < 2 else (HUB if role > 0 else -HUB)


SIDE_A = [r for r in ROLES if hub_of(r) == HUB and r != HUB]
SIDE_B = [r for r in ROLES if hub_of(r) == -HUB and r != -HUB]
SIDE_C = [r for r in ROLES if hub_of(r) == 0 and r != 0]


def dft_table():
    m = np.arange(NM)
    plane = np.arange(NZ)[:, None]
    chan = (((m // 2) % 2) * NZ + plane) * 2 + m % 2
    k = 8 * chan + m // 4
    phase = (k[:, :, None] * np.arange(FRAME)) % FRAME * (2.0 * np.pi / FRAME)
    table = np.stack([np.cos(phase), -np.sin(phase)], axis=1) / math.sqrt(FRAME)
    table = table.reshape(NZ, 2, NM // 2, 2, FRAME).transpose(0, 3, 1, 2, 4)
    return table.reshape(NZ, 2, NM, FRAME).astype(jnp.bfloat16)


def kernel(volt_hbm, proto, table_hbm, out, volt, table, vt, begun, hs, hr, filt, stage, sendp, recvp, za, zb, zc,
           pa, pb, qa, qb, fin, plane_in, insem, hsem, hrsem, psem, prsem, zsem, zrsem, qsem, qrsem, rsem, rrsem):
    grp = lax.axis_index("grp")
    chan = lax.axis_index("chan")
    core = lax.rem(chan, 2)
    z = lax.rem(chan // 2, NZ)
    ylo = chan // (2 * NZ)
    mine = grp * 4 + ylo * 2 + core
    sgn = 1 - 2 * core

    def in_plane(m, offset=0):
        return (m // 4, (lax.rem(m // 2, 2) * NZ + lax.rem(z + offset + NZ, NZ)) * 2 + lax.rem(m, 2))

    def in_column(offset):
        return (grp, (ylo * NZ + lax.rem(z + offset + 2 * NZ, NZ)) * 2 + core)

    after = (grp, lax.rem(chan + 1, 64))
    before = (grp, lax.rem(chan + 63, 64))
    beyond = (grp, lax.rem(chan + 63 + 2 * core, 64))

    fetches = [
        pltpu.make_async_copy(volt_hbm.at[n * 16:(n + 1) * 16], volt.at[n * 16:(n + 1) * 16], insem.at[n])
        for n in range(4)
    ]
    fetch_table = pltpu.make_async_copy(table_hbm, table, insem.at[4])
    for fetch in fetches:
        fetch.start()
    barrier = pltpu.get_barrier_semaphore()

    @pl.loop(1, NM)
    def _(k):
        pl.semaphore_signal(barrier, inc=1, device_id=in_plane(lax.rem(mine + k, NM)), device_id_type=MESH)

    for d in (1, 2, 3, 4, 5):
        for s in (1, -1):
            pl.semaphore_signal(barrier, inc=1, device_id=in_column(s * d), device_id_type=MESH)
    pl.semaphore_signal(barrier, inc=1, device_id=beyond, device_id_type=MESH)

    for n in range(4):
        fetches[n].wait()
        if n == 3:
            fetch_table.start()

        @pl.loop(n * 16, (n + 1) * 16)
        def _(i):
            for nt in range(8):
                tile = volt[i, :, nt * 128:(nt + 1) * 128].astype(F32)
                vt[nt, pl.ds(i, SPEC, stride=INP), :] = tile

    @pl.loop(0, 8)
    def _(nt):
        for n, f in enumerate([12, 13, 14, 15, 0, 1, 2]):
            hs[n, nt] = vt[nt, f * INP:(f + 1) * INP, :].astype(BF16)

    pl.semaphore_wait(barrier, NM - 1 + 11)
    for offset in (HUB - 7, 7 - HUB):
        pl.semaphore_signal(plane_in, inc=1, device_id=in_column(offset), device_id_type=MESH)
    forward = pltpu.make_async_remote_copy(
        src_ref=hs.at[0:BACK], dst_ref=hr.at[0:BACK], send_sem=hsem.at[0], recv_sem=hrsem.at[0],
        device_id=after, device_id_type=MESH)
    backward = pltpu.make_async_remote_copy(
        src_ref=hs.at[BACK:7], dst_ref=hr.at[BACK:7], send_sem=hsem.at[1], recv_sem=hrsem.at[1],
        device_id=before, device_id_type=MESH)
    forward.start()
    backward.start()

    last = jnp.where(chan == 63, 0.0, 1.0).astype(F32)
    first = jnp.where(chan == 0, 0.0, 1.0).astype(F32)

    def over_tiles(body):
        @pl.loop(0, 32)
        def _(idx):
            nt = idx // 4
            row = pl.multiple_of(lax.rem(idx, 4) * 16, 16)
            lanes = pl.ds(pl.multiple_of(nt * 128, 128), 128)
            body(nt, row, lanes, [proto[t:t + 1, lanes] for t in range(TAPS)])

    def own_frames(nt, row, lo, hi):
        return {f: vt[nt, pl.ds(pl.multiple_of((f - BACK) * INP + row, 16), 16), :] for f in range(lo, hi)}

    def summed(taps, frames, j):
        terms = [taps[f - j] * frames[f] for f in range(j, j + TAPS) if f in frames]
        return sum(terms[1:], terms[0])

    edge = list(range(BACK)) + list(range(SPEC - AHEAD, SPEC))

    def inner(nt, row, lanes, taps):
        frames = own_frames(nt, row, BACK, BACK + SPEC)
        for j in range(BACK, SPEC - AHEAD):
            filt[pl.ds(pl.multiple_of(j * INP + row, 16), 16), lanes] = summed(taps, frames, j).astype(BF16)

    def edge_begun(nt, row, lanes, taps):
        frames = own_frames(nt, row, BACK, BACK + SPEC)
        for n, j in enumerate(edge):
            total = summed(taps, frames, j)
            begun[n, nt, pl.ds(row, 16), :] = total if j < BACK else total * last

    def edge_ended(nt, row, lanes, taps):
        frames = {}
        for n, f in enumerate([0, 1, 2, 3, 20, 21, 22]):
            value = hr[n, nt, pl.ds(row, 16), :].astype(F32)
            frames[f] = value * first if f < BACK else value
        for n, j in enumerate(edge):
            total = begun[n, nt, pl.ds(row, 16), :] + summed(taps, frames, j)
            filt[pl.ds(pl.multiple_of(j * INP + row, 16), 16), lanes] = total.astype(BF16)

    over_tiles(inner)
    over_tiles(edge_begun)

    low = lax.broadcasted_iota(jnp.int32, (NM // 2, 128), 1) < 64

    def dft(first_u, last_u, groups):
        lhs = jnp.concatenate(
            [table[lax.rem(z + s * ROLES[u] + NZ, NZ), (s + 1) // 2] for u in range(first_u, last_u) for s in (-1, 1)],
            axis=0)
        for sg in groups:
            full = lax.dot_general(lhs, filt[sg * 256:(sg + 1) * 256, :], (((1,), (1,)), ((), ())),
                                   preferred_element_type=F32)
            for uc in range(2 * (last_u - first_u)):
                for s2 in range(2):
                    re = full[uc * 32:uc * 32 + 16, s2 * 128:(s2 + 1) * 128]
                    im = full[uc * 32 + 16:uc * 32 + 32, s2 * 128:(s2 + 1) * 128]
                    even = jnp.where(low, re, pltpu.roll(im, 64, 1))
                    odd = jnp.where(low, pltpu.roll(re, 64, 1), im)
                    row = ((first_u + uc // 2) * NM + uc % 2) * SPEC + sg * 4 + s2 * 2
                    stage[pl.ds(row, NM // 2, stride=2 * SPEC), :] = even
                    stage[pl.ds(row + 1, NM // 2, stride=2 * SPEC), :] = odd

    def pack(lo, hi):
        @pl.loop(0, NM)
        def _(m):
            for u in range(lo, hi):
                start = pl.multiple_of((u * NM + m) * SPEC, SPEC)
                sendp[u, m] = stage[pl.ds(start, SPEC), :].astype(BF16)

    def send_direct():
        pack(0, DIRECT)
        pl.semaphore_wait(plane_in, 2)

        @pl.loop(0, NM)
        def _(k):
            m = lax.rem(mine + k, NM)
            for u in range(DIRECT):
                side = 0 if ROLES[u] > 0 else 1
                slot = (SIDE_A, SIDE_B)[side].index(ROLES[u])
                offset = (1 - 2 * lax.rem(m, 2)) * (hub_of(ROLES[u]) - ROLES[u])
                pltpu.make_async_remote_copy(
                    src_ref=sendp.at[u, m], dst_ref=(za, zb)[side].at[slot, mine], send_sem=zsem,
                    recv_sem=zrsem.at[side], device_id=in_plane(m, offset), device_id_type=MESH).start()

    def send_plane(ch):
        lo, hi = CHUNKS[ch]
        pack(lo, hi)
        pltpu.make_async_copy(sendp.at[lo:hi, mine], recvp.at[lo:hi, mine], prsem.at[ch]).start()

        @pl.loop(1, NM)
        def _(k):
            m = lax.rem(mine + k, NM)
            pltpu.make_async_remote_copy(
                src_ref=sendp.at[lo:hi, m], dst_ref=recvp.at[lo:hi, mine],
                send_sem=psem, recv_sem=prsem.at[ch], device_id=in_plane(m), device_id_type=MESH).start()

    def send_column(ch):
        lo, hi = CHUNKS[ch]
        block = recvp.at[lo:hi]
        pltpu.make_async_copy(block, block, prsem.at[ch]).wait()
        for u in range(lo, hi):
            role = ROLES[u]
            hub = hub_of(role)
            if role == hub:
                continue
            side = 0 if hub > 0 else (1 if hub < 0 else 2)
            slot = (SIDE_A, SIDE_B, SIDE_C)[side].index(role)
            pltpu.make_async_remote_copy(
                src_ref=recvp.at[u], dst_ref=(za, zb, zc)[side].at[slot], send_sem=zsem, recv_sem=zrsem.at[side],
                device_id=in_column(sgn * (hub - role)), device_id_type=MESH).start()

    fetch_table.wait()
    for u in range(0, NZ, 4):
        dft(u, u + 4, (1, 2))
    forward.wait_recv()
    backward.wait_recv()

    over_tiles(edge_ended)
    dft(0, DIRECT, (0, 3))
    send_direct()
    for ch, (lo, hi) in enumerate(CHUNKS):
        dft(lo, hi, (0, 3))
        send_plane(ch)
        if ch:
            send_column(ch - 1)
    send_column(len(CHUNKS) - 1)

    flip = jnp.where(lax.broadcasted_iota(jnp.int32, (64, 128), 1) < 64, 1.0, -1.0).astype(F32)

    def group_rows(g, held, own):
        planes = held.shape[0]
        part = pl.ds(g * 4, 4)
        return jnp.concatenate(
            [held[:, part].reshape(planes * 64, 128), recvp[own, part].reshape(64, 128)], axis=0)

    def products(w, held, role, lags):
        own = ROLES.index(role)
        left = group_rows(lax.rem(grp + 1 + w, NG), held, own)
        right = [left] + [group_rows(lax.rem(grp + 1 + w - lag + NG, NG), held, own) for lag in range(1, lags)]
        full = lax.dot_general(left, jnp.concatenate(right, axis=1), (((0,), (0,)), ((), ())),
                               preferred_element_type=F32)
        blocks = []
        for lag in range(lags):
            part = full[:, lag * 128:(lag + 1) * 128]
            blocks.append(part[0:64] * flip + pltpu.roll(part[64:128], 64, 1))
        return blocks

    row = lax.broadcasted_iota(jnp.int32, (64, 128), 0)
    lane = lax.broadcasted_iota(jnp.int32, (64, 128), 1)
    left_half = lane < 64
    column = jnp.where(left_half, lane, lane - 64)

    def folded(one, two):
        lower = row >= column
        return jnp.where(left_half, jnp.where(lower, one, pltpu.roll(one, 64, 1)),
                         jnp.where(lower, pltpu.roll(two, 64, 1), two))

    def unfolded(value):
        both = jnp.where(left_half, value, pltpu.roll(value, 64, 1))
        turned = jnp.concatenate([value, value], axis=0).T[0:64]
        real = jnp.where(row >= column, both, turned)
        imag = jnp.where(row < column, both, jnp.where(row > column, -turned, 0.0))
        return jnp.where(left_half, real, imag)

    sides = ((za, HUB, pa, qa, -sgn * HUB), (zb, -HUB, pb, qb, sgn * HUB))

    def lags_of(w):
        return 5 if w < 4 else 4

    def form(pair):
        lags = lags_of(pair)
        for held, role, sums, _, _ in sides:
            diagonal = []
            for half in range(2):
                blocks = products(pair + half, held, role, lags)
                diagonal.append(blocks[0])
                for lag in range(1, lags):
                    sums[pair + half, lag - 1] = blocks[lag].astype(BF16)
            sums[pair, lags - 1] = folded(*diagonal).astype(BF16)

    def send(w):
        count = lags_of(w) - w % 2
        for side, (_, _, sums, landing, offset) in enumerate(sides):
            pltpu.make_async_remote_copy(
                src_ref=sums.at[w, 0:count], dst_ref=landing.at[w, 0:count], send_sem=qsem,
                recv_sem=qrsem.at[side, w], device_id=in_column(offset), device_id_type=MESH).start()

    scale = 1.0 / 32.0

    def reply(w):
        pltpu.make_async_remote_copy(
            src_ref=fin.at[w], dst_ref=out.at[grp], send_sem=rsem, recv_sem=rrsem.at[w],
            device_id=(lax.rem(grp + 1 + w, NG), chan), device_id_type=MESH).start()

    def finish(w):
        lags = lags_of(w)
        for side, landing in ((0, qa), (1, qb)):
            here = landing.at[w, 0:lags - w % 2]
            pltpu.make_async_copy(here, here, qrsem.at[side, w]).wait()
        for lag in range(1, lags):
            fin[w, lag] = (fin[w, lag] + qa[w, lag - 1].astype(F32) + qb[w, lag - 1].astype(F32)) * scale
        if lags == NL:
            other = fin[w, 4]
            square = jnp.concatenate([other, pltpu.roll(other, 64, 1)], axis=0)
            fin[w + 4, 4] = square.T[0:64] * flip
        if w % 2 == 0:
            packed = qa[w, lags - 1].astype(F32) + qb[w, lags - 1].astype(F32)
            fin[w, 0] = (fin[w, 0] + unfolded(packed)) * scale
            fin[w + 1, 0] = (fin[w + 1, 0] + unfolded(pltpu.roll(packed, 64, 1))) * scale
        if w < 7:
            reply(w)

    pltpu.make_async_copy(za, za, zrsem.at[0]).wait()
    pltpu.make_async_copy(zb, zb, zrsem.at[1]).wait()
    form(0)
    send(0)
    send(1)
    form(2)
    send(2)
    pltpu.make_async_copy(zc, zc, zrsem.at[2]).wait()
    for base, lags in ((0, 5), (4, 4)):
        @pl.loop(base, base + 4)
        def _(w):
            for lag, block in enumerate(products(w, zc, 0, lags)):
                fin[w, lag] = block

    for w in range(8):
        finish(w)
        if w < 5:
            if w % 2:
                form(w + 3)
            send(w + 3)
    keep = pltpu.make_async_copy(fin.at[7], out.at[grp], insem.at[0])
    keep.start()
    for w in range(7):
        here = out.at[lax.rem(grp - 1 - w + 2 * NG, NG)]
        pltpu.make_async_copy(here, here, rrsem.at[w]).wait()
    keep.wait()

    forward.wait_send()
    backward.wait_send()

    def drain(ref, sem):
        pltpu.make_async_copy(ref, ref, sem).wait()

    drain(sendp.at[DIRECT:, 0:NM - 1], psem)
    drain(recvp.at[0:len(SIDE_A) + len(SIDE_B) + len(SIDE_C)], zsem)
    for sums in (pa, pb):
        drain(sums.at[0:8, 0:4], qsem)
    drain(fin.at[0:7], rsem)


def split(packed, out, held, parts, insem, outsem):
    def fetch(n):
        return pltpu.make_async_copy(packed.at[n], held.at[n], insem.at[n])

    for n in range(NG):
        fetch(n).start()
    for n in range(NG):
        fetch(n).wait()
        value = held[n]
        parts[:, n, 0] = value[:, :, 0:64]
        parts[:, n, 1] = pltpu.roll(value, 64, 2)[:, :, 0:64]
        pltpu.make_async_copy(parts.at[:, n], out.at[0, :, n], outsem).start()
    pltpu.make_async_copy(parts, out.at[0], outsem).wait()


def shards(voltages, prototype):
    anywhere = pl.BlockSpec(memory_space=pl.ANY)
    call = pl.pallas_call(
        kernel,
        out_shape=jax.ShapeDtypeStruct((NG, NL, 64, 128), F32),
        in_specs=[anywhere, pl.BlockSpec(memory_space=pltpu.VMEM), anywhere],
        out_specs=anywhere,
        scratch_shapes=[
            pltpu.VMEM((INP, SPEC, FRAME), BF16),
            pltpu.VMEM((NZ, 2, NM, FRAME), BF16),
            pltpu.VMEM((8, SPEC * INP, 128), F32),
            pltpu.VMEM((7, 8, INP, 128), F32),
            pltpu.VMEM((7, 8, INP, 128), BF16),
            pltpu.VMEM((7, 8, INP, 128), BF16),
            pltpu.VMEM((SPEC * INP, FRAME), BF16),
            pltpu.VMEM((NZ * NM * SPEC, 128), F32),
            pltpu.VMEM((NZ, NM, SPEC, 128), BF16),
            pltpu.VMEM((NZ, NM, SPEC, 128), BF16),
            pltpu.VMEM((len(SIDE_A), NM, SPEC, 128), BF16),
            pltpu.VMEM((len(SIDE_B), NM, SPEC, 128), BF16),
            pltpu.VMEM((len(SIDE_C), NM, SPEC, 128), BF16),
            pltpu.VMEM((8, NL, 64, 128), BF16),
            pltpu.VMEM((8, NL, 64, 128), BF16),
            pltpu.VMEM((8, NL, 64, 128), BF16),
            pltpu.VMEM((8, NL, 64, 128), BF16),
            pltpu.VMEM((8, NL, 64, 128), F32),
            pltpu.SemaphoreType.REGULAR,
            pltpu.SemaphoreType.DMA((5,)),
            pltpu.SemaphoreType.DMA((2,)),
            pltpu.SemaphoreType.DMA((2,)),
            pltpu.SemaphoreType.DMA,
            pltpu.SemaphoreType.DMA((len(CHUNKS),)),
            pltpu.SemaphoreType.DMA,
            pltpu.SemaphoreType.DMA((3,)),
            pltpu.SemaphoreType.DMA,
            pltpu.SemaphoreType.DMA((2, 8)),
            pltpu.SemaphoreType.DMA,
            pltpu.SemaphoreType.DMA((7,)),
        ],
        compiler_params=pltpu.CompilerParams(
            collective_id=0, has_side_effects=True, vmem_limit_bytes=56 << 20),
        cost_estimate=pl.CostEstimate(flops=4_000_000_000, bytes_accessed=8_000_000, transcendentals=0),
        name="fx",
    )
    packed = call(voltages, prototype, jnp.asarray(dft_table()))
    return pl.pallas_call(
        split,
        out_shape=jax.ShapeDtypeStruct((1, NL, NG, 2, 64, 64), F32),
        in_specs=[anywhere],
        out_specs=anywhere,
        scratch_shapes=[
            pltpu.VMEM((NG, NL, 64, 128), F32),
            pltpu.VMEM((NL, NG, 2, 64, 64), F32),
            pltpu.SemaphoreType.DMA((NG,)),
            pltpu.SemaphoreType.DMA,
        ],
        cost_estimate=pl.CostEstimate(flops=0, bytes_accessed=4_000_000, transcendentals=0),
        name="split",
    )(packed)


def solution(mesh):
    in_specs = (P("grp", "chan", None), P())
    out_specs = P("grp", None, "chan", None, None, None)
    return jax.shard_map(shards, mesh=mesh, in_specs=in_specs, out_specs=out_specs, check_vma=False)
```

```python
import math

import jax
import jax.numpy as jnp
import numpy as np
from jax import lax
from jax.experimental import pallas as pl
from jax.experimental.pallas import tpu as pltpu
from jax.sharding import PartitionSpec as P

MESH = pl.DeviceIdType.MESH
BF16, F32 = jnp.bfloat16, jnp.float32

TAPS, FRAME, INP, SPEC = 8, 1024, 64, 16
NZ, NM, NG, NL = 16, 32, 8, 5
BACK, AHEAD = 4, 3
ROLES = [7, -7, 8, 6, -6, 5, -5, 4, -4, 2, -2, 3, -3, 1, -1, 0]
HUB = 3
DIRECT = 2
CHUNKS = ((2, 4), (4, 7), (7, 11), (11, 16))


def hub_of(role):
    return 0 if abs(role) < 2 else (HUB if role > 0 else -HUB)


SIDE_A = [r for r in ROLES if hub_of(r) == HUB and r != HUB]
SIDE_B = [r for r in ROLES if hub_of(r) == -HUB and r != -HUB]
SIDE_C = [r for r in ROLES if hub_of(r) == 0 and r != 0]


def dft_table():
    m = np.arange(NM)
    plane = np.arange(NZ)[:, None]
    chan = (((m // 2) % 2) * NZ + plane) * 2 + m % 2
    k = 8 * chan + m // 4
    phase = (k[:, :, None] * np.arange(FRAME)) % FRAME * (2.0 * np.pi / FRAME)
    table = np.stack([np.cos(phase), -np.sin(phase)], axis=1) / math.sqrt(FRAME)
    table = table.reshape(NZ, 2, NM // 2, 2, FRAME).transpose(0, 3, 1, 2, 4)
    return table.reshape(NZ, 2, NM, FRAME).astype(jnp.bfloat16)


def kernel(volt_hbm, proto, table_hbm, out, volt, table, vt, begun, hs, hr, filt, stage, sendp, recvp, za, zb, zc,
           pa, pb, qa, qb, fin, plane_in, insem, hsem, hrsem, psem, prsem, zsem, zrsem, qsem, qrsem, rsem, rrsem):
    grp = lax.axis_index("grp")
    chan = lax.axis_index("chan")
    core = lax.rem(chan, 2)
    z = lax.rem(chan // 2, NZ)
    ylo = chan // (2 * NZ)
    mine = grp * 4 + ylo * 2 + core
    sgn = 1 - 2 * core

    def in_plane(m, offset=0):
        return (m // 4, (lax.rem(m // 2, 2) * NZ + lax.rem(z + offset + NZ, NZ)) * 2 + lax.rem(m, 2))

    def in_column(offset):
        return (grp, (ylo * NZ + lax.rem(z + offset + 2 * NZ, NZ)) * 2 + core)

    after = (grp, lax.rem(chan + 1, 64))
    before = (grp, lax.rem(chan + 63, 64))
    beyond = (grp, lax.rem(chan + 63 + 2 * core, 64))

    fetches = [
        pltpu.make_async_copy(volt_hbm.at[n * 16:(n + 1) * 16], volt.at[n * 16:(n + 1) * 16], insem.at[n])
        for n in range(4)
    ]
    fetch_table = pltpu.make_async_copy(table_hbm, table, insem.at[4])
    for fetch in fetches:
        fetch.start()
    barrier = pltpu.get_barrier_semaphore()

    @pl.loop(1, NM)
    def _(k):
        pl.semaphore_signal(barrier, inc=1, device_id=in_plane(lax.rem(mine + k, NM)), device_id_type=MESH)

    for d in (1, 2, 3, 4, 5):
        for s in (1, -1):
            pl.semaphore_signal(barrier, inc=1, device_id=in_column(s * d), device_id_type=MESH)
    pl.semaphore_signal(barrier, inc=1, device_id=beyond, device_id_type=MESH)

    for n in range(4):
        fetches[n].wait()
        if n == 3:
            fetch_table.start()

        @pl.loop(n * 16, (n + 1) * 16)
        def _(i):
            for nt in range(8):
                tile = volt[i, :, nt * 128:(nt + 1) * 128].astype(F32)
                vt[nt, pl.ds(i, SPEC, stride=INP), :] = tile

    @pl.loop(0, 8)
    def _(nt):
        for n, f in enumerate([12, 13, 14, 15, 0, 1, 2]):
            hs[n, nt] = vt[nt, f * INP:(f + 1) * INP, :].astype(BF16)

    pl.semaphore_wait(barrier, NM - 1 + 11)
    for offset in (HUB - 7, 7 - HUB):
        pl.semaphore_signal(plane_in, inc=1, device_id=in_column(offset), device_id_type=MESH)
    forward = pltpu.make_async_remote_copy(
        src_ref=hs.at[0:BACK], dst_ref=hr.at[0:BACK], send_sem=hsem.at[0], recv_sem=hrsem.at[0],
        device_id=after, device_id_type=MESH)
    backward = pltpu.make_async_remote_copy(
        src_ref=hs.at[BACK:7], dst_ref=hr.at[BACK:7], send_sem=hsem.at[1], recv_sem=hrsem.at[1],
        device_id=before, device_id_type=MESH)
    forward.start()
    backward.start()

    last = jnp.where(chan == 63, 0.0, 1.0).astype(F32)
    first = jnp.where(chan == 0, 0.0, 1.0).astype(F32)

    def over_tiles(body):
        @pl.loop(0, 32)
        def _(idx):
            nt = idx // 4
            row = pl.multiple_of(lax.rem(idx, 4) * 16, 16)
            lanes = pl.ds(pl.multiple_of(nt * 128, 128), 128)
            body(nt, row, lanes, [proto[t:t + 1, lanes] for t in range(TAPS)])

    def own_frames(nt, row, lo, hi):
        return {f: vt[nt, pl.ds(pl.multiple_of((f - BACK) * INP + row, 16), 16), :] for f in range(lo, hi)}

    def summed(taps, frames, j):
        terms = [taps[f - j] * frames[f] for f in range(j, j + TAPS) if f in frames]
        return sum(terms[1:], terms[0])

    edge = list(range(BACK)) + list(range(SPEC - AHEAD, SPEC))

    def inner(nt, row, lanes, taps):
        frames = own_frames(nt, row, BACK, BACK + SPEC)
        for j in range(BACK, SPEC - AHEAD):
            filt[pl.ds(pl.multiple_of(j * INP + row, 16), 16), lanes] = summed(taps, frames, j).astype(BF16)

    def edge_begun(nt, row, lanes, taps):
        frames = own_frames(nt, row, BACK, BACK + SPEC)
        for n, j in enumerate(edge):
            total = summed(taps, frames, j)
            begun[n, nt, pl.ds(row, 16), :] = total if j < BACK else total * last

    def edge_ended(nt, row, lanes, taps):
        frames = {}
        for n, f in enumerate([0, 1, 2, 3, 20, 21, 22]):
            value = hr[n, nt, pl.ds(row, 16), :].astype(F32)
            frames[f] = value * first if f < BACK else value
        for n, j in enumerate(edge):
            total = begun[n, nt, pl.ds(row, 16), :] + summed(taps, frames, j)
            filt[pl.ds(pl.multiple_of(j * INP + row, 16), 16), lanes] = total.astype(BF16)

    over_tiles(inner)
    over_tiles(edge_begun)

    low = lax.broadcasted_iota(jnp.int32, (NM // 2, 128), 1) < 64

    def dft(first_u, last_u, groups):
        lhs = jnp.concatenate(
            [table[lax.rem(z + s * ROLES[u] + NZ, NZ), (s + 1) // 2] for u in range(first_u, last_u) for s in (-1, 1)],
            axis=0)
        for sg in groups:
            full = lax.dot_general(lhs, filt[sg * 256:(sg + 1) * 256, :], (((1,), (1,)), ((), ())),
                                   preferred_element_type=F32)
            for uc in range(2 * (last_u - first_u)):
                for s2 in range(2):
                    re = full[uc * 32:uc * 32 + 16, s2 * 128:(s2 + 1) * 128]
                    im = full[uc * 32 + 16:uc * 32 + 32, s2 * 128:(s2 + 1) * 128]
                    even = jnp.where(low, re, pltpu.roll(im, 64, 1))
                    odd = jnp.where(low, pltpu.roll(re, 64, 1), im)
                    row = ((first_u + uc // 2) * NM + uc % 2) * SPEC + sg * 4 + s2 * 2
                    stage[pl.ds(row, NM // 2, stride=2 * SPEC), :] = even
                    stage[pl.ds(row + 1, NM // 2, stride=2 * SPEC), :] = odd

    def pack(lo, hi):
        @pl.loop(0, NM)
        def _(m):
            for u in range(lo, hi):
                start = pl.multiple_of((u * NM + m) * SPEC, SPEC)
                sendp[u, m] = stage[pl.ds(start, SPEC), :].astype(BF16)

    def send_direct():
        pack(0, DIRECT)
        pl.semaphore_wait(plane_in, 2)

        @pl.loop(0, NM)
        def _(k):
            m = lax.rem(mine + k, NM)
            for u in range(DIRECT):
                side = 0 if ROLES[u] > 0 else 1
                slot = (SIDE_A, SIDE_B)[side].index(ROLES[u])
                offset = (1 - 2 * lax.rem(m, 2)) * (hub_of(ROLES[u]) - ROLES[u])
                pltpu.make_async_remote_copy(
                    src_ref=sendp.at[u, m], dst_ref=(za, zb)[side].at[slot, mine], send_sem=zsem,
                    recv_sem=zrsem.at[side], device_id=in_plane(m, offset), device_id_type=MESH).start()

    def send_plane(ch):
        lo, hi = CHUNKS[ch]
        pack(lo, hi)
        pltpu.make_async_copy(sendp.at[lo:hi, mine], recvp.at[lo:hi, mine], prsem.at[ch]).start()

        @pl.loop(1, NM)
        def _(k):
            m = lax.rem(mine + k, NM)
            pltpu.make_async_remote_copy(
                src_ref=sendp.at[lo:hi, m], dst_ref=recvp.at[lo:hi, mine],
                send_sem=psem, recv_sem=prsem.at[ch], device_id=in_plane(m), device_id_type=MESH).start()

    def send_column(ch):
        lo, hi = CHUNKS[ch]
        block = recvp.at[lo:hi]
        pltpu.make_async_copy(block, block, prsem.at[ch]).wait()
        for u in range(lo, hi):
            role = ROLES[u]
            hub = hub_of(role)
            if role == hub:
                continue
            side = 0 if hub > 0 else (1 if hub < 0 else 2)
            slot = (SIDE_A, SIDE_B, SIDE_C)[side].index(role)
            pltpu.make_async_remote_copy(
                src_ref=recvp.at[u], dst_ref=(za, zb, zc)[side].at[slot], send_sem=zsem, recv_sem=zrsem.at[side],
                device_id=in_column(sgn * (hub - role)), device_id_type=MESH).start()

    fetch_table.wait()
    for u in range(0, NZ, 4):
        dft(u, u + 4, (1, 2))
    forward.wait_recv()
    backward.wait_recv()

    over_tiles(edge_ended)
    dft(0, DIRECT, (0, 3))
    send_direct()
    for ch, (lo, hi) in enumerate(CHUNKS):
        dft(lo, hi, (0, 3))
        send_plane(ch)
        if ch:
            send_column(ch - 1)
    send_column(len(CHUNKS) - 1)

    flip = jnp.where(lax.broadcasted_iota(jnp.int32, (64, 128), 1) < 64, 1.0, -1.0).astype(F32)

    def group_rows(g, held, own):
        planes = held.shape[0]
        part = pl.ds(g * 4, 4)
        return jnp.concatenate(
            [held[:, part].reshape(planes * 64, 128), recvp[own, part].reshape(64, 128)], axis=0)

    def products(w, held, role, lags):
        own = ROLES.index(role)
        left = group_rows(lax.rem(grp + 1 + w, NG), held, own)
        right = [left] + [group_rows(lax.rem(grp + 1 + w - lag + NG, NG), held, own) for lag in range(1, lags)]
        full = lax.dot_general(left, jnp.concatenate(right, axis=1), (((0,), (0,)), ((), ())),
                               preferred_element_type=F32)
        blocks = []
        for lag in range(lags):
            part = full[:, lag * 128:(lag + 1) * 128]
            blocks.append(part[0:64] * flip + pltpu.roll(part[64:128], 64, 1))
        return blocks

    row = lax.broadcasted_iota(jnp.int32, (64, 128), 0)
    lane = lax.broadcasted_iota(jnp.int32, (64, 128), 1)
    left_half = lane < 64
    column = jnp.where(left_half, lane, lane - 64)

    def folded(one, two):
        lower = row >= column
        return jnp.where(left_half, jnp.where(lower, one, pltpu.roll(one, 64, 1)),
                         jnp.where(lower, pltpu.roll(two, 64, 1), two))

    def unfolded(value):
        both = jnp.where(left_half, value, pltpu.roll(value, 64, 1))
        turned = jnp.concatenate([value, value], axis=0).T[0:64]
        real = jnp.where(row >= column, both, turned)
        imag = jnp.where(row < column, both, jnp.where(row > column, -turned, 0.0))
        return jnp.where(left_half, real, imag)

    sides = ((za, HUB, pa, qa, -sgn * HUB), (zb, -HUB, pb, qb, sgn * HUB))

    def lags_of(w):
        return 5 if w < 4 else 4

    def form(pair):
        lags = lags_of(pair)
        for held, role, sums, _, _ in sides:
            diagonal = []
            for half in range(2):
                blocks = products(pair + half, held, role, lags)
                diagonal.append(blocks[0])
                for lag in range(1, lags):
                    sums[pair + half, lag - 1] = blocks[lag].astype(BF16)
            sums[pair, lags - 1] = folded(*diagonal).astype(BF16)

    def send(w):
        count = lags_of(w) - w % 2
        for side, (_, _, sums, landing, offset) in enumerate(sides):
            pltpu.make_async_remote_copy(
                src_ref=sums.at[w, 0:count], dst_ref=landing.at[w, 0:count], send_sem=qsem,
                recv_sem=qrsem.at[side, w], device_id=in_column(offset), device_id_type=MESH).start()

    scale = 1.0 / 32.0

    def reply(w):
        pltpu.make_async_remote_copy(
            src_ref=fin.at[w], dst_ref=out.at[grp], send_sem=rsem, recv_sem=rrsem.at[w],
            device_id=(lax.rem(grp + 1 + w, NG), chan), device_id_type=MESH).start()

    def finish(w):
        lags = lags_of(w)
        for side, landing in ((0, qa), (1, qb)):
            here = landing.at[w, 0:lags - w % 2]
            pltpu.make_async_copy(here, here, qrsem.at[side, w]).wait()
        for lag in range(1, lags):
            fin[w, lag] = (fin[w, lag] + qa[w, lag - 1].astype(F32) + qb[w, lag - 1].astype(F32)) * scale
        if lags == NL:
            other = fin[w, 4]
            square = jnp.concatenate([other, pltpu.roll(other, 64, 1)], axis=0)
            fin[w + 4, 4] = square.T[0:64] * flip
        if w % 2 == 0:
            packed = qa[w, lags - 1].astype(F32) + qb[w, lags - 1].astype(F32)
            fin[w, 0] = (fin[w, 0] + unfolded(packed)) * scale
            fin[w + 1, 0] = (fin[w + 1, 0] + unfolded(pltpu.roll(packed, 64, 1))) * scale
        if w < 7:
            reply(w)

    pltpu.make_async_copy(za, za, zrsem.at[0]).wait()
    pltpu.make_async_copy(zb, zb, zrsem.at[1]).wait()
    form(0)
    send(0)
    send(1)
    form(2)
    send(2)
    pltpu.make_async_copy(zc, zc, zrsem.at[2]).wait()
    for base, lags in ((0, 5), (4, 4)):
        @pl.loop(base, base + 4)
        def _(w):
            for lag, block in enumerate(products(w, zc, 0, lags)):
                fin[w, lag] = block

    for w in range(8):
        finish(w)
        if w < 5:
            if w % 2:
                form(w + 3)
            send(w + 3)
    keep = pltpu.make_async_copy(fin.at[7], out.at[grp], insem.at[0])
    keep.start()
    for w in range(7):
        here = out.at[lax.rem(grp - 1 - w + 2 * NG, NG)]
        pltpu.make_async_copy(here, here, rrsem.at[w]).wait()
    keep.wait()

    forward.wait_send()
    backward.wait_send()

    def drain(ref, sem):
        pltpu.make_async_copy(ref, ref, sem).wait()

    drain(sendp.at[DIRECT:, 0:NM - 1], psem)
    drain(recvp.at[0:len(SIDE_A) + len(SIDE_B) + len(SIDE_C)], zsem)
    for sums in (pa, pb):
        drain(sums.at[0:8, 0:4], qsem)
    drain(fin.at[0:7], rsem)


def split(packed, out, held, parts, insem, outsem):
    def fetch(n):
        return pltpu.make_async_copy(packed.at[n], held.at[n], insem.at[n])

    for n in range(NG):
        fetch(n).start()
    for n in range(NG):
        fetch(n).wait()
        value = held[n]
        parts[:, n, 0] = value[:, :, 0:64]
        parts[:, n, 1] = pltpu.roll(value, 64, 2)[:, :, 0:64]
        pltpu.make_async_copy(parts.at[:, n], out.at[0, :, n], outsem).start()
    pltpu.make_async_copy(parts, out.at[0], outsem).wait()


def shards(voltages, prototype):
    anywhere = pl.BlockSpec(memory_space=pl.ANY)
    call = pl.pallas_call(
        kernel,
        out_shape=jax.ShapeDtypeStruct((NG, NL, 64, 128), F32),
        in_specs=[anywhere, pl.BlockSpec(memory_space=pltpu.VMEM), anywhere],
        out_specs=anywhere,
        scratch_shapes=[
            pltpu.VMEM((INP, SPEC, FRAME), BF16),
            pltpu.VMEM((NZ, 2, NM, FRAME), BF16),
            pltpu.VMEM((8, SPEC * INP, 128), F32),
            pltpu.VMEM((7, 8, INP, 128), F32),
            pltpu.VMEM((7, 8, INP, 128), BF16),
            pltpu.VMEM((7, 8, INP, 128), BF16),
            pltpu.VMEM((SPEC * INP, FRAME), BF16),
            pltpu.VMEM((NZ * NM * SPEC, 128), F32),
            pltpu.VMEM((NZ, NM, SPEC, 128), BF16),
            pltpu.VMEM((NZ, NM, SPEC, 128), BF16),
            pltpu.VMEM((len(SIDE_A), NM, SPEC, 128), BF16),
            pltpu.VMEM((len(SIDE_B), NM, SPEC, 128), BF16),
            pltpu.VMEM((len(SIDE_C), NM, SPEC, 128), BF16),
            pltpu.VMEM((8, NL, 64, 128), BF16),
            pltpu.VMEM((8, NL, 64, 128), BF16),
            pltpu.VMEM((8, NL, 64, 128), BF16),
            pltpu.VMEM((8, NL, 64, 128), BF16),
            pltpu.VMEM((8, NL, 64, 128), F32),
            pltpu.SemaphoreType.REGULAR,
            pltpu.SemaphoreType.DMA((5,)),
            pltpu.SemaphoreType.DMA((2,)),
            pltpu.SemaphoreType.DMA((2,)),
            pltpu.SemaphoreType.DMA,
            pltpu.SemaphoreType.DMA((len(CHUNKS),)),
            pltpu.SemaphoreType.DMA,
            pltpu.SemaphoreType.DMA((3,)),
            pltpu.SemaphoreType.DMA,
            pltpu.SemaphoreType.DMA((2, 8)),
            pltpu.SemaphoreType.DMA,
            pltpu.SemaphoreType.DMA((7,)),
        ],
        compiler_params=pltpu.CompilerParams(
            collective_id=0, has_side_effects=True, vmem_limit_bytes=56 << 20),
        cost_estimate=pl.CostEstimate(flops=4_000_000_000, bytes_accessed=8_000_000, transcendentals=0),
        name="fx",
    )
    packed = call(voltages, prototype, jnp.asarray(dft_table()))
    return pl.pallas_call(
        split,
        out_shape=jax.ShapeDtypeStruct((1, NL, NG, 2, 64, 64), F32),
        in_specs=[anywhere],
        out_specs=anywhere,
        scratch_shapes=[
            pltpu.VMEM((NG, NL, 64, 128), F32),
            pltpu.VMEM((NL, NG, 2, 64, 64), F32),
            pltpu.SemaphoreType.DMA((NG,)),
            pltpu.SemaphoreType.DMA,
        ],
        cost_estimate=pl.CostEstimate(flops=0, bytes_accessed=4_000_000, transcendentals=0),
        name="split",
    )(packed)


def solution(mesh):
    in_specs = (P("grp", "chan", None), P())
    out_specs = P("grp", None, "chan", None, None, None)
    return jax.shard_map(shards, mesh=mesh, in_specs=in_specs, out_specs=out_specs, check_vma=False)
```
